128 devices in a mesh: expert: 16 (over x, z), shard: 8 (over y, core).
Axes of the slice: x: 4, y: 4, z: 4, core: 2. Of those that a mesh axis runs over, the one named last changes fastest.
Arguments:
- hidden_in: bfloat16 [16384, 2048], P(('expert', 'shard')), may hold values from -6 to 6
- cotangent: bfloat16 [16384, 2048], P(('expert', 'shard')), may hold values from -6 to 6
- lengths: int32 [16, 3], P('expert'), may hold values from 1 to 768, 1024 in all within a row
- dealing: int32 [16, 1024], P('expert'), may hold values from 0 to 1023, each once within a row
- routes: int32 [16384, 2], P(('expert', 'shard')), may hold values from 0 to 63, all different within a row; in each aligned block of 128 rows (0 to 127, 128 to 255, ...) at most 5 rows name the same one
- norm_attn: bfloat16 [2048], P(('expert', 'shard')), may hold values from 0.099609375 to 1.8984375
- w_query: bfloat16 [2048, 3072], P(('expert', 'shard')), may hold values from -0.1875 to 0.1875
- w_latent: bfloat16 [2048, 576], P(('expert', 'shard')), may hold values from -0.125 to 0.125
- norm_latent: bfloat16 [512], P(('expert', 'shard')), may hold values from 0.099609375 to 1.8984375
- w_expand: bfloat16 [512, 4096], P(('expert', 'shard')), may hold values from -0.25 to 0.25
- w_out: bfloat16 [2048, 2048], P(('expert', 'shard')), may hold values from -1 to 1
- norm_ffn: bfloat16 [2048], P(('expert', 'shard')), may hold values from 0.099609375 to 1.8984375
- w_router: bfloat16 [2048, 64], P(('expert', 'shard')), may hold values from -0.0625 to 0.0625
- w_shared_gate: bfloat16 [2048, 1408], P(('expert', 'shard')), may hold values from -0.125 to 0.125
- w_shared_up: bfloat16 [2048, 1408], P(('expert', 'shard')), may hold values from -0.125 to 0.125
- w_shared_down: bfloat16 [1408, 2048], P(('expert', 'shard')), may hold values from -0.15625 to 0.15625
- w_expert_gate: bfloat16 [64, 1408, 2048], P('expert', 'shard'), may hold values from -0.125 to 0.125
- w_expert_up: bfloat16 [64, 1408, 2048], P('expert', 'shard'), may hold values from -0.125 to 0.125
- w_expert_down: bfloat16 [64, 1408, 2048], P('expert', 'shard'), may hold values from -0.15625 to 0.15625
Outputs:
- layer_out: bfloat16 [16384, 2048], P(('expert', 'shard'))
- grad_input: float32 [16384, 2048], P(('expert', 'shard'))
- grad_norm_attn: float32 [2048], P(('expert', 'shard'))
- grad_query: float32 [2048, 3072], P(('expert', 'shard'))
- grad_latent: float32 [2048, 576], P(('expert', 'shard'))
- grad_norm_latent: float32 [512], P(('expert', 'shard'))
- grad_expand: float32 [512, 4096], P(('expert', 'shard'))
- grad_out: float32 [2048, 2048], P(('expert', 'shard'))
- grad_norm_ffn: float32 [2048], P(('expert', 'shard'))
- grad_router: float32 [2048, 64], P(('expert', 'shard'))
- grad_shared_gate: float32 [2048, 1408], P(('expert', 'shard'))
- grad_shared_up: float32 [2048, 1408], P(('expert', 'shard'))
- grad_shared_down: float32 [1408, 2048], P(('expert', 'shard'))
- grad_expert_gate: float32 [64, 1408, 2048], P('expert', 'shard')
- grad_expert_up: float32 [64, 1408, 2048], P('expert', 'shard')
- grad_expert_down: float32 [64, 1408, 2048], P('expert', 'shard')
The draws below stay inside these ranges and needn't reach their ends.
Inputs may be any that keep to these rules, and one draw needn't show every extreme that they name: Each group's 3 lengths sum to 1024, and one of them is exactly 768. `dealing`: each row holds every place 0 to 1023 once. `routes`: a token names 2 different experts; among the rows of one device no expert is named more than 5 times, and 5 is reached.
All inputs are finite; a program needn't handle non-finite values.
Results may differ from the reference program's by a relative error of at most 0.03.
Values may be sent and summed in bfloat16 or wider, within the bound.
No kernel may reach another device: no remote copies, remote signals or barrier semaphores. Data moves between devices by JAX's collectives and lax.ppermute only.
A program may use at most 384 MiB of HBM per device.

```python
import math
from functools import partial
import jax
import jax.numpy as jnp
import numpy as np
from jax import lax

D = 2048
H = 16
DN = 128
DR = 64
DV = 128
R = 512
FE = 1408
FS = 1408
TOPK = 2
SEQS = 3
TOK_DEV = 128
EXPERTS = 64
GROUP_TOK = 1024
MAXLEN = 768
CAP = 5
TOKENS = 16384
N_EXPERT = 16
N_SHARD = 8


def block_scale(key, dims, pieces, low, high):
    loudness = 1.0
    for dim, blocks in pieces:
        draws = jax.random.uniform(jax.random.fold_in(jax.random.fold_in(key, 6), dim), (blocks,), jnp.float32, low / len(pieces), high / len(pieces))
        loudness = loudness * jnp.repeat(jnp.exp(draws), dims[dim] // blocks).reshape((-1,) + (1,) * (len(dims) - 1 - dim))
    return loudness


def profile(count, total, bound, lean):
    portions = [(1 << 20) // math.isqrt(standing ** lean) + 1 for standing in range(2, count + 1)]
    surplus, holding = total - bound - (count - 1), [1] * (count - 1)
    while surplus > 0:
        free = [i for i in range(count - 1) if holding[i] < bound]
        whole, budget = sum([portions[i] for i in free]), surplus
        for i in free:
            more = min(bound - holding[i], max(1, budget * portions[i] // whole), surplus)
            holding[i] = holding[i] + more
            surplus = surplus - more
    return np.array([bound] + holding)


def ragged(rng, count, total, most, lean):
    if count == 2:
        one = jax.random.randint(rng, (), max(1, total - most), min(most, total - 1) + 1)
        return jnp.stack([one, total - one])
    sizes = jnp.asarray(profile(count, total, most, lean), jnp.int32)
    couples = (count - 1) // 2
    donor, receiver = sizes[1:1 + 2 * couples:2], sizes[2:2 + 2 * couples:2]
    slack = jnp.minimum(donor - 1, most - receiver)
    moved = jax.random.randint(jax.random.fold_in(rng, 1), (couples,), 0, 1 << 20) % (slack + 1)
    sizes = sizes.at[1:1 + 2 * couples:2].set(donor - moved).at[2:2 + 2 * couples:2].set(receiver + moved)
    return sizes[jax.random.permutation(jax.random.fold_in(rng, 2), count)]


def deal_out(stream_key, own, number, rows, number_of, top, reach, lean):
    order = jax.random.permutation(stream_key, number_of)
    crowded, usual = shares(number_of, rows * top, reach, lean, True), shares(number_of, rows * top, reach, lean, False)
    places = jnp.arange(number_of)

    def named(sizes, rotation):
        used = int((sizes > 0).sum())
        fixed = max(1, used // 4)
        moved = fixed + (places - fixed + rotation * (used - fixed)) % max(1, number_of - fixed)
        return jnp.zeros((number_of,), jnp.int32).at[order[jnp.where(places < fixed, places, moved)]].set(jnp.asarray(sizes, jnp.int32))

    sizes = jnp.where(number % 4 == 0, named(crowded, number // 4), named(usual, number - number // 4 - 1))
    mixed = jax.random.permutation(jax.random.fold_in(own, 3), number_of)
    giver, sink = mixed[0:number_of // 2 * 2:2], mixed[1:number_of // 2 * 2:2]
    room = jnp.minimum(sizes[giver] - 1, reach - sizes[sink]) // 2
    room = jnp.where((giver == order[0]) | (sink == order[0]) | (sizes[sink] == 0), 0, jnp.maximum(room, 0))
    moved = jax.random.randint(jax.random.fold_in(own, 4), (number_of // 2,), 0, 1 << 20) % (room + 1)
    sizes = sizes.at[giver].add(-moved).at[sink].add(moved)
    labels = jnp.searchsorted(jnp.cumsum(sizes), jnp.arange(rows * top), side="right").astype(jnp.int32)
    listing = labels.reshape(top, rows).T
    listing = listing[jax.random.permutation(jax.random.fold_in(own, 1), rows)]
    rotation = jax.random.randint(jax.random.fold_in(own, 2), (rows, 1), 0, top)
    return jnp.take_along_axis(listing, (jnp.arange(top)[None, :] + rotation) % top, axis=1)


def shares(number_of, total, bound, lean, full):
    weights = [(1 << 20) // math.isqrt(grade ** lean) + 1 for grade in range(1, number_of + 1)]
    largest = bound if full else min(bound, max(-(-total // number_of), total * weights[0] // sum(weights)))
    least = 1 if total - largest >= number_of - 1 else 0
    counts, spare = [largest] + [least] * (number_of - 1), total - largest - least * (number_of - 1)
    while spare > 0:
        free = [i for i in range(1, number_of) if counts[i] < largest] or [i for i in range(1, number_of) if counts[i] < bound]
        whole, remaining = sum([weights[i] for i in free]), spare
        for i in free:
            addition = min(bound - counts[i], max(1, remaining * weights[i] // whole), spare)
            counts[i] = counts[i] + addition
            spare = spare - addition
    return np.array(counts)


def centred(key, extent, scale, limit, pieces=(), held_as=jnp.bfloat16):
    array = jax.random.normal(key, extent, jnp.float32) * scale
    if len(pieces) > 0:
        array = block_scale(key, extent, pieces, -0.22, 0.18) * array
    return jnp.clip(array, min=-limit, max=limit).astype(held_as)


def setup_inputs(seed: int = 0) -> dict:
    key_of = jax.random.split(jax.random.key(seed), 20)
    hidden_in = centred(key_of[0], (TOKENS, D), 1.0, 6.0, ((0, 128),))
    cotangent = centred(key_of[1], (TOKENS, D), 1.0, 6.0, ((0, 128),))
    lengths = jax.vmap(lambda own: ragged(own, SEQS, GROUP_TOK, MAXLEN, 2))(jax.random.split(key_of[2], N_EXPERT)).reshape((N_EXPERT, SEQS)).astype(jnp.int32)
    dealing = jax.vmap(lambda own: jax.random.permutation(own, GROUP_TOK))(jax.random.split(key_of[3], N_EXPERT)).reshape((N_EXPERT, GROUP_TOK)).astype(jnp.int32)
    routes_keys = jax.random.split(jax.random.fold_in(key_of[4], 1), TOKENS // TOK_DEV)
    routes_turns = jax.random.permutation(jax.random.fold_in(key_of[4], 3), TOKENS // TOK_DEV)
    routes = jax.vmap(lambda own, number: deal_out(jax.random.fold_in(key_of[4], 2), own, number, TOK_DEV, EXPERTS, TOPK, CAP, 2))(routes_keys, routes_turns).reshape((TOKENS, TOPK))
    norm_attn = jnp.clip(1.0 + 0.18 * jax.random.normal(key_of[5], (D,), jnp.float32), 0.099609375, 1.8984375).astype(jnp.bfloat16)
    w_query = centred(key_of[6], (D, H * (DN + DR)), (D // 2) ** -0.5, 0.1875, ((0, 128),))
    w_latent = centred(key_of[7], (D, R + DR), D ** -0.5, 0.125, ((0, 128),))
    norm_latent = jnp.clip(1.0 + 0.18 * jax.random.normal(key_of[8], (R,), jnp.float32), 0.099609375, 1.8984375).astype(jnp.bfloat16)
    w_expand = centred(key_of[9], (R, H * (DN + DV)), R ** -0.5, 0.25, ((0, 128),))
    w_out = centred(key_of[10], (H * DV, D), (H * DV // 64) ** -0.5, 1.0, ((0, 128),))
    norm_ffn = jnp.clip(1.0 + 0.18 * jax.random.normal(key_of[11], (D,), jnp.float32), 0.099609375, 1.8984375).astype(jnp.bfloat16)
    w_router = centred(key_of[12], (D, EXPERTS), (4 * D) ** -0.5, 0.0625, ((0, 128),))
    w_shared_gate = centred(key_of[13], (D, FS), D ** -0.5, 0.125, ((0, 128),))
    w_shared_up = centred(key_of[14], (D, FS), D ** -0.5, 0.125, ((0, 128),))
    w_shared_down = centred(key_of[15], (FS, D), FS ** -0.5, 0.15625, ((0, 128),))
    w_expert_gate = centred(key_of[16], (EXPERTS, FE, D), D ** -0.5, 0.125, ((0, 16), (1, 8)))
    w_expert_up = centred(key_of[17], (EXPERTS, FE, D), D ** -0.5, 0.125, ((0, 16), (1, 8)))
    w_expert_down = centred(key_of[18], (EXPERTS, FE, D), FE ** -0.5, 0.15625, ((0, 16), (1, 8)))
    return dict(hidden_in=hidden_in, cotangent=cotangent, lengths=lengths, dealing=dealing, routes=routes, norm_attn=norm_attn, w_query=w_query, w_latent=w_latent, norm_latent=norm_latent, w_expand=w_expand, w_out=w_out, norm_ffn=norm_ffn, w_router=w_router, w_shared_gate=w_shared_gate, w_shared_up=w_shared_up, w_shared_down=w_shared_down, w_expert_gate=w_expert_gate, w_expert_up=w_expert_up, w_expert_down=w_expert_down)


@jax.custom_vjp
def low(v):
    return lax.optimization_barrier(v.astype(jnp.bfloat16)).astype(jnp.float32)

@jax.custom_vjp
def low_back(v):
    return v

def low_keep(v):
    return (low(v), None)

def low_pass(kept, grad):
    return (grad,)

def back_keep(v):
    return (v, None)

def back_low(kept, grad):
    return (low(grad),)
low.defvjp(low_keep, low_pass)
low_back.defvjp(back_keep, back_low)
EPSILON = 1e-06
ROPE_BASE = 50000.0
ROUTE_SCALE = 2.446
MASKED = -1e+30
HIGHEST = lax.Precision.HIGHEST

def matmul(left, right):
    return jnp.dot(left, right, precision=HIGHEST, preferred_element_type=jnp.float32)

def matmul_nt(left, right):
    return lax.dot_general(left, right, (((1,), (1,)), ((), ())), precision=HIGHEST, preferred_element_type=jnp.float32)

def rms_scale(value, gain):
    return value * lax.rsqrt(lax.optimization_barrier(jnp.mean(value * value, axis=-1, keepdims=True)) + EPSILON) * gain

def rope_tables(position, width):
    half_width = width // 2
    rates = ROPE_BASE ** (-2.0 * jnp.arange(half_width, dtype=jnp.float32) / width)
    angles = position.astype(jnp.float32)[:, None] * rates[None, :]
    return (jnp.cos(angles), jnp.sin(angles))

def rotate(value, cosine, sine_table):
    half_width = value.shape[-1] // 2
    front_half = value[..., :half_width]
    back_half = value[..., half_width:]
    return jnp.concatenate([front_half * cosine - back_half * sine_table, back_half * cosine + front_half * sine_table], axis=-1)

def attend_group(inputs):
    queries, expanded, key_rope, places, segment = inputs
    key_count = key_rope.shape[0]
    keys = jnp.concatenate([expanded[..., :DN], jnp.broadcast_to(key_rope[:, None, :], (key_count, H, DR))], axis=-1)
    scores = low_back(jnp.einsum('qhc,khc->hqk', queries, keys, precision=HIGHEST) * (DN + DR) ** (-0.5))
    allowed = (segment[:, None] == segment[None, :]) & (places[None, :] <= places[:, None])
    masked = jnp.where(allowed[None], scores, MASKED)
    row_peak = lax.optimization_barrier(jnp.max(masked, axis=-1, keepdims=True))
    weights = jnp.exp(masked - row_peak)
    attention_probs = weights / lax.optimization_barrier(jnp.sum(weights, axis=-1, keepdims=True))
    return jnp.einsum('hqk,khv->qhv', low(attention_probs), expanded[..., DN:], precision=HIGHEST)

def expert_block(normed_mid, inputs):
    gate_w, up_w, down_w, source = inputs
    rows_in = low_back(jnp.take(normed_mid, source // TOPK, axis=0))
    gate_pre = low_back(matmul_nt(rows_in, gate_w))
    up_pre = low_back(matmul_nt(rows_in, up_w))
    expert_hidden = low(jax.nn.silu(gate_pre) * up_pre)
    return low(low_back(matmul(expert_hidden, down_w)))

def layer(inputs32, norm_attn, w_query, w_latent, norm_latent, w_expand, w_out, norm_ffn, w_router, w_shared_gate, w_shared_up, w_shared_down, w_expert_gate, w_expert_up, w_expert_down, tables):
    places, segment, cosine, sine_table, routes, slot_source, slot_live = tables
    normed_in = low(rms_scale(inputs32, norm_attn))
    query_proj = low_back(matmul(normed_in, w_query)).reshape(TOKENS, H, DN + DR)
    latent = low_back(matmul(normed_in, w_latent))
    latent_normed = low(rms_scale(latent[:, :R], norm_latent))
    expanded = low(low_back(matmul(latent_normed, w_expand))).reshape(TOKENS, H, DN + DV)
    key_rope = low(rotate(latent[:, R:], cosine, sine_table))
    queries = low(jnp.concatenate([query_proj[..., :DN], rotate(query_proj[..., DN:], cosine[:, None, :], sine_table[:, None, :])], axis=-1))
    groups = (queries.reshape(N_EXPERT, GROUP_TOK, H, DN + DR), expanded.reshape(N_EXPERT, GROUP_TOK, H, DN + DV), key_rope.reshape(N_EXPERT, GROUP_TOK, DR), places, segment)
    mixed_heads = lax.map(jax.checkpoint(attend_group), groups)
    attended = low(low_back(mixed_heads.reshape(TOKENS, H * DV)))
    middle = inputs32 + low_back(matmul(attended, w_out))
    normed_mid = low(rms_scale(middle, norm_ffn))
    logits = low_back(matmul(normed_mid, w_router))
    chosen = jnp.take_along_axis(logits, routes, axis=1)
    scores_sig = jax.nn.sigmoid(chosen)
    gate_values = ROUTE_SCALE * scores_sig / lax.optimization_barrier(jnp.sum(scores_sig, axis=1, keepdims=True))
    shared_a = low_back(matmul(normed_mid, w_shared_gate))
    shared_b = low_back(matmul(normed_mid, w_shared_up))
    shared_out = low_back(matmul(low(jax.nn.silu(shared_a) * shared_b), w_shared_down))
    expert_out = lax.map(jax.checkpoint(partial(expert_block, normed_mid)), (w_expert_gate, w_expert_up, w_expert_down, slot_source))
    slot_gate = jnp.take(gate_values.reshape(-1), slot_source, axis=0) * slot_live
    weighted = (expert_out * slot_gate[..., None]).reshape(-1, expert_out.shape[-1])
    mixture = jnp.zeros_like(middle).at[(slot_source // TOPK).reshape(-1)].add(weighted)
    return middle + shared_out + mixture

def reference(hidden_in, cotangent, lengths, dealing, routes, norm_attn, w_query, w_latent, norm_latent, w_expand, w_out, norm_ffn, w_router, w_shared_gate, w_shared_up, w_shared_down, w_expert_gate, w_expert_up, w_expert_down):
    places = dealing.astype(jnp.int32)
    seq_ends = jnp.cumsum(lengths, axis=1).astype(jnp.int32)
    seq_starts = (seq_ends - lengths).astype(jnp.int32)
    segment = lax.optimization_barrier(jnp.sum((places[:, :, None] >= seq_ends[:, None, :]).astype(jnp.int32), axis=2)).astype(jnp.int32)
    seq_ids = jnp.arange(SEQS, dtype=jnp.int32)
    start_of = lax.optimization_barrier(jnp.sum(jnp.where(segment[:, :, None] == seq_ids[None, None, :], seq_starts[:, None, :], 0), axis=2)).astype(jnp.int32)
    position = (places - start_of).reshape(-1).astype(jnp.int32)
    cosine, sine_table = rope_tables(position, DR)
    flat_expert = routes.reshape(-1).astype(jnp.int32)
    flat_hot = (flat_expert[:, None] == jnp.arange(EXPERTS, dtype=jnp.int32)[None, :]).astype(jnp.int32)
    slot_rank = (lax.optimization_barrier(jnp.sum(flat_hot * jnp.cumsum(flat_hot, axis=0), axis=1)) - 1).astype(jnp.int32)
    slot_total = CAP * N_EXPERT * N_SHARD
    route_ids = jnp.arange(TOKENS * TOPK, dtype=jnp.int32)
    slot_source = jnp.zeros((EXPERTS, slot_total), jnp.int32).at[flat_expert, slot_rank].set(route_ids)
    slot_live = jnp.zeros((EXPERTS, slot_total), jnp.float32).at[flat_expert, slot_rank].set(1.0)
    tables = (places, segment, cosine, sine_table, routes.astype(jnp.int32), slot_source, slot_live)
    floats = [value.astype(jnp.float32) for value in (hidden_in, norm_attn, w_query, w_latent, norm_latent, w_expand, w_out, norm_ffn, w_router, w_shared_gate, w_shared_up, w_shared_down, w_expert_gate, w_expert_up, w_expert_down)]
    output, pullback = jax.vjp(lambda *params: layer(*params, tables), *floats)
    grads = pullback(cotangent.astype(jnp.float32))
    return (output.astype(jnp.bfloat16), grads[0], grads[1], grads[2], grads[3], grads[4], grads[5], grads[6], grads[7], grads[8], grads[9], grads[10], grads[11], grads[12], grads[13], grads[14])
```

```python
import jax
import jax.numpy as jnp
from jax import lax
from jax.experimental import pallas as pl
from jax.experimental.pallas import tpu as pltpu
from jax.sharding import PartitionSpec as P

H = 16
DN = 128
DR = 64
DV = 128
R = 512
EXP_DEV = 4
TOPK = 2
CAP = 5
N_EXPERT = 16
N_SHARD = 8
SLOT = 24
HEADS = H // N_SHARD
QW = HEADS * (DN + DR)
KVW = HEADS * (DN + DV)
LW = R + DR

EPSILON = 1e-06
ROPE_BASE = 50000.0
ROUTE_SCALE = 2.446
MASKED = -1e30
BF = jnp.bfloat16
F32 = jnp.float32


def product(left, right):
    return jnp.dot(left, right, preferred_element_type=F32)


def product_tn(left, right):
    return lax.dot_general(left, right, (((0,), (0,)), ((), ())), preferred_element_type=F32)


def product_nt(left, right):
    return lax.dot_general(left, right, (((1,), (1,)), ((), ())), preferred_element_type=F32)


def rms_forward(value, gain):
    inverse = lax.rsqrt(jnp.mean(value * value, axis=-1, keepdims=True) + EPSILON)
    return (value * inverse * gain, inverse)


def rms_backward(value, inverse, gain, grad):
    weighted = grad * gain
    inner = jnp.mean(weighted * value, axis=-1, keepdims=True)
    value_grad = inverse * weighted - value * (inverse * inverse * inverse) * inner
    return (value_grad, jnp.sum(grad * value * inverse, axis=0))


def rope_tables(position, width):
    half_width = width // 2
    rates = ROPE_BASE ** (-2.0 * jnp.arange(half_width, dtype=F32) / width)
    angles = position.astype(F32)[:, None] * rates[None, :]
    return (jnp.cos(angles), jnp.sin(angles))


def rotate(value, cosine, sine_table):
    half_width = value.shape[-1] // 2
    front_half = value[..., :half_width]
    back_half = value[..., half_width:]
    return jnp.concatenate(
        [
            front_half * cosine - back_half * sine_table,
            back_half * cosine + front_half * sine_table,
        ],
        axis=-1,
    )


def silu_parts(value):
    logistic = jax.nn.sigmoid(value)
    return (value * logistic, logistic * (1.0 + value * (1.0 - logistic)))


def turn_pairs():
    pairs = []
    for e in range(N_EXPERT):
        for s in range(N_SHARD):
            pairs.append((e * N_SHARD + s, (N_SHARD * (e % 2) + s) * N_SHARD + e // 2))
    return pairs


def in_order(first, then):
    return lax.optimization_barrier((first, then))


def zero_after(*firsts):
    total = 0.0
    for first in firsts:
        tile = first.reshape(-1, first.shape[-1])[:8, :128]
        total = jnp.maximum(total, jnp.max(tile.astype(F32)))
    return jnp.where(total != total, total, 0.0)


def peek_kernel(tile_ref, before_ref, zero_ref):
    tile = tile_ref[...].astype(F32) + before_ref[0]
    zero_ref[...] = jnp.where(tile != tile, tile, 0.0)


def peek(first, before=None):
    flat = first.reshape(-1, first.shape[-1])
    if before is None:
        before = jnp.zeros((), F32)
    zeros = pl.pallas_call(
        peek_kernel,
        grid=(1,),
        in_specs=[
            pl.BlockSpec((16, 128), lambda i: (0, 0)),
            pl.BlockSpec(memory_space=pltpu.SMEM),
        ],
        out_specs=pl.BlockSpec((16, 128), lambda i: (0, 0)),
        out_shape=jax.ShapeDtypeStruct((16, 128), F32),
        cost_estimate=pl.CostEstimate(flops=4096, bytes_accessed=12288, transcendentals=0),
    )(flat, before.reshape(1))
    return zeros[:8]


def owner_grads_kernel(normed_ref, grad_ref, expand_ref, gain_ref, head_ref, latent_ref):
    acc = product_nt(normed_ref[...].T, grad_ref[...]).astype(BF)
    head_ref[0, :, :QW] = acc[:, :QW]
    head_ref[0, :, QW:] = expand_ref[0]
    gain = gain_ref[0].astype(BF)
    for s in range(N_SHARD):
        own = slice(16 * s, 16 * s + 16)
        latent_ref[s, :, :R] = acc[own, QW : QW + R]
        latent_ref[s, :, R:] = gain[own]
        latent_ref[s, :, R:LW] = acc[own, QW + R :]


def owner_grads(normed, grad, expand, gain):
    tokens = normed.shape[0]
    return pl.pallas_call(
        owner_grads_kernel,
        grid=(N_EXPERT,),
        in_specs=[
            pl.BlockSpec((tokens, 128), lambda i: (0, i)),
            pl.BlockSpec((QW + LW, tokens), lambda i: (0, 0)),
            pl.BlockSpec((1, 128, 128), lambda i: (i, 0, 0)),
            pl.BlockSpec((1, 128, 128), lambda i: (i, 0, 0)),
        ],
        out_specs=[
            pl.BlockSpec((1, 128, QW + 128), lambda i: (i, 0, 0)),
            pl.BlockSpec((N_SHARD, 16, 640), lambda i: (0, i, 0)),
        ],
        out_shape=[
            jax.ShapeDtypeStruct((N_EXPERT, 128, QW + 128), BF),
            jax.ShapeDtypeStruct((N_SHARD, N_EXPERT * 16, 640), BF),
        ],
        compiler_params=pltpu.CompilerParams(vmem_limit_bytes=24 * 1024 * 1024),
        cost_estimate=pl.CostEstimate(
            flops=2 * tokens * 2048 * 960, bytes_accessed=12 * 1024 * 1024, transcendentals=0
        ),
    )(normed, grad.T, expand, gain)


def in_turn(then, *firsts):
    return then + zero_after(*firsts).astype(then.dtype)


def sum_over_expert(pieces):
    got = lax.all_to_all(pieces, "expert", split_axis=0, concat_axis=0, tiled=True)
    return jnp.sum(got.astype(F32), axis=0)


def to_owners(pieces):
    got = lax.all_to_all(
        pieces, ("expert", "shard"), split_axis=0, concat_axis=0, tiled=True
    )
    return got.reshape((N_EXPERT, N_SHARD) + pieces.shape[1:]).astype(F32)


def body(
    hidden_in,
    cotangent,
    lengths,
    dealing,
    routes,
    norm_attn,
    w_query,
    w_latent,
    norm_latent,
    w_expand,
    w_out,
    norm_ffn,
    w_router,
    w_shared_gate,
    w_shared_up,
    w_shared_down,
    w_expert_gate,
    w_expert_up,
    w_expert_down,
):
    rows, width = hidden_in.shape
    group = rows * N_SHARD
    expert_count = EXP_DEV * N_EXPERT
    factor = (DN + DR) ** (-0.5)
    hid = w_shared_gate.shape[1] // N_SHARD
    my_shard = lax.axis_index("shard")
    my_first = my_shard * rows
    pairs = turn_pairs()
    back_pairs = [(b, a) for a, b in pairs]

    def spread(block):
        return jnp.broadcast_to(block[None], (N_SHARD,) + block.shape)

    def split_columns(block):
        return block.reshape(16, N_SHARD, -1).transpose(1, 0, 2)

    x_group = lax.all_gather(hidden_in, "shard", axis=0, tiled=True)
    latent_gain16 = jnp.pad(norm_latent, (0, 12))
    gains = jnp.stack([norm_attn, norm_ffn, latent_gain16], axis=1)
    expand_block = w_expand.reshape(4, N_SHARD, KVW // 128, 128).transpose(1, 0, 2, 3)
    columns = jnp.concatenate(
        [
            split_columns(w_query),
            spread(w_latent),
            expand_block.reshape(N_SHARD, 16, 128),
            spread(jnp.pad(gains, ((0, 0), (0, 61)))),
            spread(w_router),
            jnp.zeros((N_SHARD, 16, 64), BF),
            split_columns(w_shared_gate),
            split_columns(w_shared_up),
        ],
        axis=2,
    ).reshape(N_SHARD * 16, 1280 + 2 * hid)
    columns = lax.all_to_all(columns, "shard", split_axis=0, concat_axis=0, tiled=True)
    turned = lax.ppermute(
        jnp.concatenate([w_out, w_shared_down, jnp.zeros((5, width), BF)], axis=0),
        ("expert", "shard"),
        pairs,
    )
    weights = lax.all_gather(
        in_turn(
            jnp.concatenate([columns[:, :1280], turned[:16].reshape(128, 256)], axis=1), x_group
        ),
        "expert",
        axis=0,
        tiled=True,
    )

    place = dealing[0]
    seq_lengths = lengths[0]
    seq_ends = jnp.cumsum(seq_lengths)
    seq_starts = seq_ends - seq_lengths
    seq_ids = jnp.arange(seq_lengths.shape[0], dtype=jnp.int32)
    segment = jnp.sum((place[:, None] >= seq_ends[None, :]).astype(jnp.int32), axis=1)
    start = jnp.sum(
        jnp.where(segment[:, None] == seq_ids[None, :], seq_starts[None, :], 0), axis=1
    )
    cosine, sine = rope_tables(place - start, DR)
    allowed = (place[None, :] <= place[:, None]) & (place[None, :] >= start[:, None])

    flat_expert = routes.reshape(-1)
    earlier = jnp.arange(rows * TOPK)
    same = (flat_expert[:, None] == flat_expert[None, :]) & (earlier[None, :] < earlier[:, None])
    rank = jnp.sum(same.astype(jnp.int32), axis=1)
    slot = (
        (flat_expert // EXP_DEV) * SLOT + (flat_expert % EXP_DEV) * CAP + rank
    ).reshape(rows, TOPK)
    slot_ids = jnp.arange(N_EXPERT * SLOT, dtype=jnp.int32)
    hot = [(slot[:, k][:, None] == slot_ids[None, :]) for k in range(TOPK)]
    hot_any = (hot[0] | hot[1]).astype(BF)
    own_rows = EXP_DEV * N_EXPERT * CAP
    ids = jnp.arange(own_rows, dtype=jnp.int32)
    by_source = (
        (ids % (N_EXPERT * CAP)) // CAP * SLOT + ids // (N_EXPERT * CAP) * CAP + ids % CAP
    )
    deal = (by_source[:, None] == slot_ids[None, :]).astype(BF)

    def to_owner(packed):
        arrived = lax.all_to_all(packed, "expert", split_axis=0, concat_axis=0, tiled=True)
        return product(deal, arrived).astype(BF).reshape(EXP_DEV, N_EXPERT * CAP, width)

    def from_owner(own):
        packed = product_tn(deal, own.reshape(own_rows, width)).astype(BF)
        return lax.all_to_all(packed, "expert", split_axis=0, concat_axis=0, tiled=True)

    own_cot = to_owner(product_tn(hot_any, in_turn(cotangent, columns)).astype(BF))
    weights, own_cot = in_order(weights, own_cot)
    expert_cot = lax.all_gather(own_cot, "shard", axis=1, tiled=True)
    query_latent_w = weights[:, : QW + LW]
    query_w = weights[:, :QW]
    latent_w = weights[:, QW : QW + LW]
    expand_w = weights[:, 960:1088].reshape(R, KVW)
    gain_attn = weights[:, 1088].astype(F32)
    gain_ffn = weights[:, 1089].astype(F32)
    gain_latent = weights[:, 1090].reshape(128, 16)[:, :4].reshape(R).astype(F32)
    router_w = weights[:, 1152 : 1152 + expert_count]
    out_w = weights[:, 1280:].reshape(N_EXPERT * 16, width)

    ffn_sent = jnp.concatenate([columns[:, 1280:], turned[16:27].reshape(128, hid)], axis=1)
    ffn_sent = jnp.broadcast_to(
        in_turn(ffn_sent, weights)[None], (N_EXPERT,) + ffn_sent.shape
    ).reshape(N_EXPERT * 128, 3 * hid)
    ffn_w = lax.all_to_all(ffn_sent, "expert", split_axis=0, concat_axis=0, tiled=True)
    gate_up_w = ffn_w[:, : 2 * hid]
    down_w = ffn_w[:, 2 * hid :].reshape(hid, width)

    x_all = x_group.astype(F32)
    normed_f, _ = rms_forward(x_all, gain_attn)
    normed_in = normed_f.astype(BF)
    projected = product(normed_in, query_latent_w)
    compressed = projected[:, QW : QW + R]
    latent_f, _ = rms_forward(compressed, gain_latent)
    latent_normed = latent_f.astype(BF)
    expanded = product(latent_normed, expand_w).astype(BF)
    key_rope = rotate(projected[:, QW + R :], cosine, sine).astype(BF)
    queries = []
    keys = []
    values = []
    for h in range(HEADS):
        q_h = projected[:, h * (DN + DR) : (h + 1) * (DN + DR)]
        queries.append(
            jnp.concatenate([q_h[:, :DN], rotate(q_h[:, DN:], cosine, sine)], axis=1).astype(BF)
        )
        kv_h = expanded[:, h * (DN + DV) : (h + 1) * (DN + DV)]
        keys.append(jnp.concatenate([kv_h[:, :DN], key_rope], axis=1))
        values.append(kv_h[:, DN:])
    probs_low = []
    mixed = []
    for h in range(HEADS):
        masked = jnp.where(allowed, product_nt(queries[h], keys[h]) * factor, MASKED)
        peak = jnp.max(masked, axis=-1, keepdims=True)
        raised = jnp.exp(masked - peak)
        probs = raised / jnp.sum(raised, axis=-1, keepdims=True)
        probs_low.append(probs.astype(BF))
        mixed.append(product(probs_low[h], values[h]))
    attended = jnp.concatenate(mixed, axis=1).astype(BF)
    attended = in_turn(attended, peek(expert_cot), ffn_w)
    out_part = product(attended, out_w).astype(BF)
    out_own = lax.psum_scatter(out_part, "shard", scatter_dimension=0, tiled=True)
    w_expert_both = jnp.concatenate([w_expert_gate, w_expert_up], axis=1)
    out_own = in_turn(out_own, peek(w_expert_both))
    inputs32 = hidden_in.astype(F32)
    middle = inputs32 + out_own.astype(F32)
    mid_f, inverse_mid = rms_forward(middle, gain_ffn)
    normed_mid = mid_f.astype(BF)

    logits = product(normed_mid, router_w)
    route_hot = (
        routes[:, :, None] == jnp.arange(expert_count, dtype=jnp.int32)[None, None, :]
    ).astype(F32)
    chosen = jnp.sum(route_hot * logits[:, None, :], axis=-1)
    scores_sig = jax.nn.sigmoid(chosen)
    sig_total = jnp.sum(scores_sig, axis=1, keepdims=True)
    gate_values = ROUTE_SCALE * scores_sig / sig_total
    slot_gate = sum(
        jnp.sum(jnp.where(hot[k], gate_values[:, k][:, None], 0.0), axis=0) for k in range(TOPK)
    )

    own_sent = to_owner(product_tn(hot_any, normed_mid).astype(BF))
    mid_group = lax.all_gather(normed_mid, "shard", axis=0, tiled=True)
    mid_group, own_sent = in_order(mid_group, own_sent)
    expert_rows = lax.all_gather(own_sent, "shard", axis=1, tiled=True)
    gate_rows = jnp.broadcast_to(
        slot_gate.reshape(N_EXPERT, 1, SLOT)[:, :, : EXP_DEV * CAP],
        (N_EXPERT, N_SHARD, EXP_DEV * CAP),
    ).reshape(N_EXPERT * N_SHARD, EXP_DEV * CAP)
    gate_rows = lax.all_to_all(
        gate_rows, ("expert", "shard"), split_axis=0, concat_axis=0, tiled=True
    )
    gate_rows = (
        gate_rows.reshape(N_EXPERT, N_SHARD, EXP_DEV, CAP)
        .transpose(2, 1, 0, 3)
        .reshape(EXP_DEV, N_SHARD * N_EXPERT * CAP, 1)
    )

    mid_sent = in_turn(mid_group, gate_rows)
    shared_ab = product(mid_sent, gate_up_w)
    shared_a = shared_ab[:, :hid]
    shared_b = shared_ab[:, hid:]
    silu_shared, slope_shared = silu_parts(shared_a)
    shared_hidden = (silu_shared * shared_b).astype(BF)
    shared_part = product(shared_hidden, down_w).astype(BF)
    expert_first, cot_sent = in_order(
        zero_after(peek(expert_rows, zero_after(gate_rows, shared_part))), cotangent
    )
    cot_group = lax.all_gather(cot_sent, "shard", axis=0, tiled=True)

    both_pre = jnp.einsum("jsd,jfd->jsf", expert_rows, w_expert_both, preferred_element_type=F32)
    gate_pre = both_pre[..., :hid]
    up_pre = both_pre[..., hid:]
    silu_gate, slope_gate = silu_parts(gate_pre)
    expert_hidden = (silu_gate * up_pre).astype(BF)
    expert_hidden = expert_hidden + expert_first.astype(BF)
    hidden_grad = gate_rows * jnp.einsum(
        "jsd,jfd->jsf", expert_cot, w_expert_down, preferred_element_type=F32
    )
    gate_part = jnp.sum(expert_hidden.astype(F32) * hidden_grad, axis=-1)
    grad_gate_pre = (hidden_grad * up_pre * slope_gate).astype(BF)
    grad_up_pre = (hidden_grad * silu_gate).astype(BF)
    row_part = jnp.einsum(
        "jsf,jfd->jsd",
        jnp.concatenate([grad_gate_pre, grad_up_pre], axis=2),
        w_expert_both,
        preferred_element_type=F32,
    ).astype(BF)
    row_own = lax.psum_scatter(row_part, "shard", scatter_dimension=1, tiled=True)
    gate_sent = (
        gate_part.reshape(EXP_DEV, N_SHARD, N_EXPERT, CAP)
        .transpose(2, 1, 0, 3)
        .reshape(N_EXPERT * N_SHARD, EXP_DEV * CAP)
    )
    gate_got = lax.all_to_all(
        gate_sent, ("expert", "shard"), split_axis=0, concat_axis=0, tiled=True
    )
    gate_sum = jnp.sum(gate_got.reshape(N_EXPERT, N_SHARD, EXP_DEV * CAP), axis=1)
    gate_slots = jnp.pad(gate_sum, ((0, 0), (0, SLOT - EXP_DEV * CAP))).reshape(-1)
    gate_times_grad = jnp.stack(
        [jnp.sum(jnp.where(hot[k], gate_slots[None, :], 0.0), axis=1) for k in range(TOPK)], axis=1
    )

    gate_total = jnp.sum(gate_times_grad, axis=1, keepdims=True)
    chosen_grad = (gate_times_grad - gate_values * (gate_total / ROUTE_SCALE)) * (
        1.0 - scores_sig
    )
    logit_grad = jnp.sum(route_hot * chosen_grad[:, :, None], axis=1).astype(BF)

    shared_hidden_grad = product_nt(cot_group, down_w)
    grad_shared_ab = jnp.concatenate(
        [shared_hidden_grad * shared_b * slope_shared, shared_hidden_grad * silu_shared], axis=1
    ).astype(BF)
    shared_row_part = product_nt(grad_shared_ab, gate_up_w).astype(BF)
    gate_up_sum = sum_over_expert(
        jnp.concatenate(
            [
                product_tn(mid_sent, grad_shared_ab).astype(BF),
                product_tn(normed_mid, logit_grad).astype(BF),
            ],
            axis=1,
        ).reshape(N_EXPERT, 128, 2 * hid + expert_count)
    )
    row_own = in_turn(row_own, gate_got, gate_up_sum)
    row_own, shared_row_part = in_order(row_own, shared_row_part)
    shared_row = lax.psum_scatter(shared_row_part, "shard", scatter_dimension=0, tiled=True)
    row_back = from_owner(row_own)

    grad_routes = product(hot_any.astype(BF), row_back)
    grad_top = cotangent.astype(F32)
    normed_grad = product_nt(logit_grad, router_w) + shared_row.astype(F32) + grad_routes
    middle_norm_grad, grad_gain_ffn = rms_backward(middle, inverse_mid, gain_ffn, normed_grad)
    middle_grad = grad_top + middle_norm_grad
    attn_grad = middle_grad.astype(BF)
    grad_group = lax.all_gather(attn_grad, "shard", axis=0, tiled=True)
    ffn_got = lax.all_to_all(
        in_turn(gate_up_sum, attn_grad).astype(BF),
        "shard",
        split_axis=0,
        concat_axis=0,
        tiled=True,
    )
    ffn_got = ffn_got.reshape(N_SHARD, 16, 2 * hid + expert_count).astype(F32)
    expert_part = jnp.einsum(
        "jsf,jfd->jsd",
        in_turn(expert_hidden, attn_grad),
        w_expert_down,
        preferred_element_type=F32,
    ).astype(BF)
    expert_own = lax.psum_scatter(expert_part, "shard", scatter_dimension=1, tiled=True)
    mixed = [in_turn(one, expert_part, ffn_got) for one in mixed]

    attended_grad = product_nt(grad_group, out_w).astype(BF)
    out_sum = sum_over_expert(
        product_tn(attended, grad_group)
        .astype(BF)
        .reshape(N_EXPERT, 16, width)
    )
    query_grads = []
    expanded_grads = []
    rope_grad = 0.0
    for h in range(HEADS):
        a_h = attended_grad[:, h * DV : (h + 1) * DV]
        inner = in_turn(jnp.sum(mixed[h] * a_h.astype(F32), axis=-1, keepdims=True), out_sum)
        probs_grad = product_nt(a_h, values[h])
        score_grad = (probs_low[h].astype(F32) * (probs_grad - inner)).astype(BF)
        value_grad = product_tn(probs_low[h], a_h)
        query_grad = product(score_grad, keys[h]) * factor
        key_grad = product_tn(score_grad, queries[h]) * factor
        query_grads.append(query_grad[:, :DN])
        query_grads.append(rotate(query_grad[:, DN:], cosine, -sine))
        expanded_grads.append(key_grad[:, :DN])
        expanded_grads.append(value_grad)
        rope_grad = rope_grad + key_grad[:, DN:]
    down_sum = sum_over_expert(
        jnp.pad(
            product_tn(in_turn(shared_hidden, out_sum, rope_grad), cot_group)
            .astype(BF)
            .reshape(N_EXPERT, 11, width),
            ((0, 0), (0, 5), (0, 0)),
        )
    )
    expanded_grad = jnp.concatenate(expanded_grads, axis=1).astype(BF)
    inverse_latent = lax.rsqrt(
        jnp.mean(compressed * compressed, axis=-1, keepdims=True) + EPSILON
    )
    compressed_grad, _ = rms_backward(
        compressed, inverse_latent, gain_latent, product_nt(expanded_grad, expand_w)
    )
    projected_grad = jnp.concatenate(
        query_grads + [compressed_grad, rotate(rope_grad, cosine, -sine)], axis=1
    ).astype(BF)

    ffn_gain = jnp.pad(grad_gain_ffn.reshape(N_EXPERT, 128, 1), ((0, 0), (0, 0), (64, 63)))
    normed_part = product_nt(projected_grad, query_latent_w).astype(BF)
    expert_own, normed_part = in_order(expert_own, normed_part)
    normed_in_grad = lax.psum_scatter(normed_part, "shard", scatter_dimension=0, tiled=True)
    grads_sent, latent_sent = owner_grads(
        normed_in,
        projected_grad,
        product_tn(latent_normed, expanded_grad).astype(BF).reshape(N_EXPERT, 128, 128),
        in_turn(ffn_gain, normed_part, down_sum),
    )
    grads_sum = sum_over_expert(grads_sent)
    latent_own = lax.psum_scatter(
        latent_sent.reshape(N_SHARD * N_EXPERT * 16, 640),
        "shard",
        scatter_dimension=0,
        tiled=True,
    )
    normed_in_grad, shared_part = in_order(normed_in_grad, shared_part)
    shared_out = lax.psum_scatter(shared_part, "shard", scatter_dimension=0, tiled=True)
    grads_got = lax.all_to_all(
        grads_sum.astype(BF), "shard", split_axis=0, concat_axis=0, tiled=True
    )
    grads_got = grads_got.reshape(N_SHARD, 16, QW + 128).astype(F32)
    latent_sum = sum_over_expert(latent_own.reshape(N_EXPERT, 16, 640))
    turned_back = lax.ppermute(
        in_turn(jnp.concatenate([out_sum, down_sum], axis=0), grads_sum).astype(BF),
        ("expert", "shard"),
        back_pairs,
    ).astype(F32)

    grad_expert_down = jnp.einsum(
        "jsf,jsd->jfd",
        in_turn((expert_hidden.astype(F32) * gate_rows).astype(BF), grads_sent),
        expert_cot,
        preferred_element_type=F32,
    )
    grad_expert_gate = jnp.einsum(
        "jsf,jsd->jfd",
        in_turn(grad_gate_pre, grads_sent),
        expert_rows,
        preferred_element_type=F32,
    )
    grad_expert_up = jnp.einsum(
        "jsf,jsd->jfd",
        in_turn(grad_up_pre, grads_sent),
        expert_rows,
        preferred_element_type=F32,
    )

    normed_in_grad = normed_in_grad.astype(F32)
    inverse_in = lax.rsqrt(jnp.mean(inputs32 * inputs32, axis=-1, keepdims=True) + EPSILON)
    input_norm_grad, _ = rms_backward(
        inputs32, inverse_in, gain_attn, normed_in_grad
    )
    grad_input = middle_grad + input_norm_grad

    expert_back = from_owner(expert_own)
    route_out = [product(hot[k].astype(BF), expert_back) for k in range(TOPK)]
    mixture = sum(gate_values[:, k][:, None] * route_out[k] for k in range(TOPK))
    layer_out = (middle + shared_out.astype(F32) + mixture).astype(BF)

    grad_shared_gate = ffn_got[:, :, :hid].transpose(1, 0, 2).reshape(16, N_SHARD * hid)
    grad_shared_up = (
        ffn_got[:, :, hid : 2 * hid].transpose(1, 0, 2).reshape(16, N_SHARD * hid)
    )
    grad_router_own = jnp.sum(ffn_got[:, :, 2 * hid :], axis=0)
    grad_shared_down = turned_back[16:27]
    grad_out_own = turned_back[:16]

    query_own = grads_got[:, :, :QW].transpose(1, 0, 2).reshape(16, N_SHARD * QW)
    grad_expand_own = (
        grads_got[:, :, QW : QW + 128]
        .reshape(N_SHARD, 4, KVW // 128, 128)
        .transpose(1, 0, 2, 3)
        .reshape(4, N_SHARD * KVW)
    )
    grad_latent_own = latent_sum[:, :LW]
    grad_norm_ffn = latent_sum[:, LW]
    grad_norm_attn = (
        jnp.sum(w_query.astype(F32) * query_own, axis=1)
        + jnp.sum(w_latent.astype(F32) * grad_latent_own, axis=1)
    ) / norm_attn.astype(F32)
    grad_norm_latent = jnp.sum(w_expand.astype(F32) * grad_expand_own, axis=1) / (
        norm_latent.astype(F32)
    )

    return (
        layer_out,
        grad_input,
        grad_norm_attn,
        query_own,
        grad_latent_own,
        grad_norm_latent,
        grad_expand_own,
        grad_out_own,
        grad_norm_ffn,
        grad_router_own,
        grad_shared_gate,
        grad_shared_up,
        grad_shared_down,
        grad_expert_gate,
        grad_expert_up,
        grad_expert_down,
    )


def solution(mesh):
    both = P(("expert", "shard"), None)
    vector = P(("expert", "shard"))
    groups = P("expert", None)
    experts = P("expert", "shard", None)
    return jax.shard_map(
        body,
        mesh=mesh,
        in_specs=(
            both,
            both,
            groups,
            groups,
            both,
            vector,
            both,
            both,
            vector,
            both,
            both,
            vector,
            both,
            both,
            both,
            both,
            experts,
            experts,
            experts,
        ),
        out_specs=(
            both,
            both,
            vector,
            both,
            both,
            vector,
            both,
            both,
            vector,
            both,
            both,
            both,
            both,
            experts,
            experts,
            experts,
        ),
        check_vma=False,
    )
```

```python
import jax
import jax.numpy as jnp
from jax import lax
from jax.experimental import pallas as pl
from jax.experimental.pallas import tpu as pltpu
from jax.sharding import PartitionSpec as P

H = 16
DN = 128
DR = 64
DV = 128
R = 512
EXP_DEV = 4
TOPK = 2
CAP = 5
N_EXPERT = 16
N_SHARD = 8
SLOT = 24
HEADS = H // N_SHARD
QW = HEADS * (DN + DR)
KVW = HEADS * (DN + DV)
LW = R + DR

EPSILON = 1e-06
ROPE_BASE = 50000.0
ROUTE_SCALE = 2.446
MASKED = -1e30
BF = jnp.bfloat16
F32 = jnp.float32


def product(left, right):
    return jnp.dot(left, right, preferred_element_type=F32)


def product_tn(left, right):
    return lax.dot_general(left, right, (((0,), (0,)), ((), ())), preferred_element_type=F32)


def product_nt(left, right):
    return lax.dot_general(left, right, (((1,), (1,)), ((), ())), preferred_element_type=F32)


def rms_forward(value, gain):
    inverse = lax.rsqrt(jnp.mean(value * value, axis=-1, keepdims=True) + EPSILON)
    return (value * inverse * gain, inverse)


def rms_backward(value, inverse, gain, grad):
    weighted = grad * gain
    inner = jnp.mean(weighted * value, axis=-1, keepdims=True)
    value_grad = inverse * weighted - value * (inverse * inverse * inverse) * inner
    return (value_grad, jnp.sum(grad * value * inverse, axis=0))


def rope_tables(position, width):
    half_width = width // 2
    rates = ROPE_BASE ** (-2.0 * jnp.arange(half_width, dtype=F32) / width)
    angles = position.astype(F32)[:, None] * rates[None, :]
    return (jnp.cos(angles), jnp.sin(angles))


def rotate(value, cosine, sine_table):
    half_width = value.shape[-1] // 2
    front_half = value[..., :half_width]
    back_half = value[..., half_width:]
    return jnp.concatenate(
        [
            front_half * cosine - back_half * sine_table,
            back_half * cosine + front_half * sine_table,
        ],
        axis=-1,
    )


def silu_parts(value):
    logistic = jax.nn.sigmoid(value)
    return (value * logistic, logistic * (1.0 + value * (1.0 - logistic)))


def turn_pairs():
    pairs = []
    for e in range(N_EXPERT):
        for s in range(N_SHARD):
            pairs.append((e * N_SHARD + s, (N_SHARD * (e % 2) + s) * N_SHARD + e // 2))
    return pairs


def in_order(first, then):
    return lax.optimization_barrier((first, then))


def zero_after(*firsts):
    total = 0.0
    for first in firsts:
        tile = first.reshape(-1, first.shape[-1])[:8, :128]
        total = jnp.maximum(total, jnp.max(tile.astype(F32)))
    return jnp.where(total != total, total, 0.0)


def peek_kernel(tile_ref, before_ref, zero_ref):
    tile = tile_ref[...].astype(F32) + before_ref[0]
    zero_ref[...] = jnp.where(tile != tile, tile, 0.0)


def peek(first, before=None):
    flat = first.reshape(-1, first.shape[-1])
    if before is None:
        before = jnp.zeros((), F32)
    zeros = pl.pallas_call(
        peek_kernel,
        grid=(1,),
        in_specs=[
            pl.BlockSpec((16, 128), lambda i: (0, 0)),
            pl.BlockSpec(memory_space=pltpu.SMEM),
        ],
        out_specs=pl.BlockSpec((16, 128), lambda i: (0, 0)),
        out_shape=jax.ShapeDtypeStruct((16, 128), F32),
        cost_estimate=pl.CostEstimate(flops=4096, bytes_accessed=12288, transcendentals=0),
    )(flat, before.reshape(1))
    return zeros[:8]


def owner_grads_kernel(normed_ref, grad_ref, expand_ref, gain_ref, head_ref, latent_ref):
    acc = product_nt(normed_ref[...].T, grad_ref[...]).astype(BF)
    head_ref[0, :, :QW] = acc[:, :QW]
    head_ref[0, :, QW:] = expand_ref[0]
    gain = gain_ref[0].astype(BF)
    for s in range(N_SHARD):
        own = slice(16 * s, 16 * s + 16)
        latent_ref[s, :, :R] = acc[own, QW : QW + R]
        latent_ref[s, :, R:] = gain[own]
        latent_ref[s, :, R:LW] = acc[own, QW + R :]


def owner_grads(normed, grad, expand, gain):
    tokens = normed.shape[0]
    return pl.pallas_call(
        owner_grads_kernel,
        grid=(N_EXPERT,),
        in_specs=[
            pl.BlockSpec((tokens, 128), lambda i: (0, i)),
            pl.BlockSpec((QW + LW, tokens), lambda i: (0, 0)),
            pl.BlockSpec((1, 128, 128), lambda i: (i, 0, 0)),
            pl.BlockSpec((1, 128, 128), lambda i: (i, 0, 0)),
        ],
        out_specs=[
            pl.BlockSpec((1, 128, QW + 128), lambda i: (i, 0, 0)),
            pl.BlockSpec((N_SHARD, 16, 640), lambda i: (0, i, 0)),
        ],
        out_shape=[
            jax.ShapeDtypeStruct((N_EXPERT, 128, QW + 128), BF),
            jax.ShapeDtypeStruct((N_SHARD, N_EXPERT * 16, 640), BF),
        ],
        compiler_params=pltpu.CompilerParams(vmem_limit_bytes=24 * 1024 * 1024),
        cost_estimate=pl.CostEstimate(
            flops=2 * tokens * 2048 * 960, bytes_accessed=12 * 1024 * 1024, transcendentals=0
        ),
    )(normed, grad.T, expand, gain)


def in_turn(then, *firsts):
    return then + zero_after(*firsts).astype(then.dtype)


def sum_over_expert(pieces):
    got = lax.all_to_all(pieces, "expert", split_axis=0, concat_axis=0, tiled=True)
    return jnp.sum(got.astype(F32), axis=0)


def to_owners(pieces):
    got = lax.all_to_all(
        pieces, ("expert", "shard"), split_axis=0, concat_axis=0, tiled=True
    )
    return got.reshape((N_EXPERT, N_SHARD) + pieces.shape[1:]).astype(F32)


def body(
    hidden_in,
    cotangent,
    lengths,
    dealing,
    routes,
    norm_attn,
    w_query,
    w_latent,
    norm_latent,
    w_expand,
    w_out,
    norm_ffn,
    w_router,
    w_shared_gate,
    w_shared_up,
    w_shared_down,
    w_expert_gate,
    w_expert_up,
    w_expert_down,
):
    rows, width = hidden_in.shape
    group = rows * N_SHARD
    expert_count = EXP_DEV * N_EXPERT
    factor = (DN + DR) ** (-0.5)
    hid = w_shared_gate.shape[1] // N_SHARD
    my_shard = lax.axis_index("shard")
    my_first = my_shard * rows
    pairs = turn_pairs()
    back_pairs = [(b, a) for a, b in pairs]

    def spread(block):
        return jnp.broadcast_to(block[None], (N_SHARD,) + block.shape)

    def split_columns(block):
        return block.reshape(16, N_SHARD, -1).transpose(1, 0, 2)

    x_group = lax.all_gather(hidden_in, "shard", axis=0, tiled=True)
    latent_gain16 = jnp.pad(norm_latent, (0, 12))
    gains = jnp.stack([norm_attn, norm_ffn, latent_gain16], axis=1)
    expand_block = w_expand.reshape(4, N_SHARD, KVW // 128, 128).transpose(1, 0, 2, 3)
    columns = jnp.concatenate(
        [
            split_columns(w_query),
            spread(w_latent),
            expand_block.reshape(N_SHARD, 16, 128),
            spread(jnp.pad(gains, ((0, 0), (0, 61)))),
            spread(w_router),
            jnp.zeros((N_SHARD, 16, 64), BF),
            split_columns(w_shared_gate),
            split_columns(w_shared_up),
        ],
        axis=2,
    ).reshape(N_SHARD * 16, 1280 + 2 * hid)
    columns = lax.all_to_all(columns, "shard", split_axis=0, concat_axis=0, tiled=True)
    turned = lax.ppermute(
        jnp.concatenate([w_out, w_shared_down, jnp.zeros((5, width), BF)], axis=0),
        ("expert", "shard"),
        pairs,
    )
    weights = lax.all_gather(
        in_turn(
            jnp.concatenate([columns[:, :1280], turned[:16].reshape(128, 256)], axis=1), x_group
        ),
        "expert",
        axis=0,
        tiled=True,
    )

    place = dealing[0]
    seq_lengths = lengths[0]
    seq_ends = jnp.cumsum(seq_lengths)
    seq_starts = seq_ends - seq_lengths
    seq_ids = jnp.arange(seq_lengths.shape[0], dtype=jnp.int32)
    segment = jnp.sum((place[:, None] >= seq_ends[None, :]).astype(jnp.int32), axis=1)
    start = jnp.sum(
        jnp.where(segment[:, None] == seq_ids[None, :], seq_starts[None, :], 0), axis=1
    )
    cosine, sine = rope_tables(place - start, DR)
    allowed = (place[None, :] <= place[:, None]) & (place[None, :] >= start[:, None])

    flat_expert = routes.reshape(-1)
    earlier = jnp.arange(rows * TOPK)
    same = (flat_expert[:, None] == flat_expert[None, :]) & (earlier[None, :] < earlier[:, None])
    rank = jnp.sum(same.astype(jnp.int32), axis=1)
    slot = (
        (flat_expert // EXP_DEV) * SLOT + (flat_expert % EXP_DEV) * CAP + rank
    ).reshape(rows, TOPK)
    slot_ids = jnp.arange(N_EXPERT * SLOT, dtype=jnp.int32)
    hot = [(slot[:, k][:, None] == slot_ids[None, :]) for k in range(TOPK)]
    hot_any = (hot[0] | hot[1]).astype(BF)
    own_rows = EXP_DEV * N_EXPERT * CAP
    ids = jnp.arange(own_rows, dtype=jnp.int32)
    by_source = (
        (ids % (N_EXPERT * CAP)) // CAP * SLOT + ids // (N_EXPERT * CAP) * CAP + ids % CAP
    )
    deal = (by_source[:, None] == slot_ids[None, :]).astype(BF)

    def to_owner(packed):
        arrived = lax.all_to_all(packed, "expert", split_axis=0, concat_axis=0, tiled=True)
        return product(deal, arrived).astype(BF).reshape(EXP_DEV, N_EXPERT * CAP, width)

    def from_owner(own):
        packed = product_tn(deal, own.reshape(own_rows, width)).astype(BF)
        return lax.all_to_all(packed, "expert", split_axis=0, concat_axis=0, tiled=True)

    own_cot = to_owner(product_tn(hot_any, in_turn(cotangent, columns)).astype(BF))
    weights, own_cot = in_order(weights, own_cot)
    expert_cot = lax.all_gather(own_cot, "shard", axis=1, tiled=True)
    query_latent_w = weights[:, : QW + LW]
    query_w = weights[:, :QW]
    latent_w = weights[:, QW : QW + LW]
    expand_w = weights[:, 960:1088].reshape(R, KVW)
    gain_attn = weights[:, 1088].astype(F32)
    gain_ffn = weights[:, 1089].astype(F32)
    gain_latent = weights[:, 1090].reshape(128, 16)[:, :4].reshape(R).astype(F32)
    router_w = weights[:, 1152 : 1152 + expert_count]
    out_w = weights[:, 1280:].reshape(N_EXPERT * 16, width)

    ffn_sent = jnp.concatenate([columns[:, 1280:], turned[16:27].reshape(128, hid)], axis=1)
    ffn_sent = jnp.broadcast_to(
        in_turn(ffn_sent, weights)[None], (N_EXPERT,) + ffn_sent.shape
    ).reshape(N_EXPERT * 128, 3 * hid)
    ffn_w = lax.all_to_all(ffn_sent, "expert", split_axis=0, concat_axis=0, tiled=True)
    gate_up_w = ffn_w[:, : 2 * hid]
    down_w = ffn_w[:, 2 * hid :].reshape(hid, width)

    x_all = x_group.astype(F32)
    normed_f, _ = rms_forward(x_all, gain_attn)
    normed_in = normed_f.astype(BF)
    projected = product(normed_in, query_latent_w)
    compressed = projected[:, QW : QW + R]
    latent_f, _ = rms_forward(compressed, gain_latent)
    latent_normed = latent_f.astype(BF)
    expanded = product(latent_normed, expand_w).astype(BF)
    key_rope = rotate(projected[:, QW + R :], cosine, sine).astype(BF)
    queries = []
    keys = []
    values = []
    for h in range(HEADS):
        q_h = projected[:, h * (DN + DR) : (h + 1) * (DN + DR)]
        queries.append(
            jnp.concatenate([q_h[:, :DN], rotate(q_h[:, DN:], cosine, sine)], axis=1).astype(BF)
        )
        kv_h = expanded[:, h * (DN + DV) : (h + 1) * (DN + DV)]
        keys.append(jnp.concatenate([kv_h[:, :DN], key_rope], axis=1))
        values.append(kv_h[:, DN:])
    probs_low = []
    mixed = []
    for h in range(HEADS):
        masked = jnp.where(allowed, product_nt(queries[h], keys[h]) * factor, MASKED)
        peak = jnp.max(masked, axis=-1, keepdims=True)
        raised = jnp.exp(masked - peak)
        probs = raised / jnp.sum(raised, axis=-1, keepdims=True)
        probs_low.append(probs.astype(BF))
        mixed.append(product(probs_low[h], values[h]))
    attended = jnp.concatenate(mixed, axis=1).astype(BF)
    attended = in_turn(attended, peek(expert_cot), ffn_w)
    out_part = product(attended, out_w).astype(BF)
    out_own = lax.psum_scatter(out_part, "shard", scatter_dimension=0, tiled=True)
    w_expert_both = jnp.concatenate([w_expert_gate, w_expert_up], axis=1)
    out_own = in_turn(out_own, peek(w_expert_both))
    inputs32 = hidden_in.astype(F32)
    middle = inputs32 + out_own.astype(F32)
    mid_f, inverse_mid = rms_forward(middle, gain_ffn)
    normed_mid = mid_f.astype(BF)

    logits = product(normed_mid, router_w)
    route_hot = (
        routes[:, :, None] == jnp.arange(expert_count, dtype=jnp.int32)[None, None, :]
    ).astype(F32)
    chosen = jnp.sum(route_hot * logits[:, None, :], axis=-1)
    scores_sig = jax.nn.sigmoid(chosen)
    sig_total = jnp.sum(scores_sig, axis=1, keepdims=True)
    gate_values = ROUTE_SCALE * scores_sig / sig_total
    slot_gate = sum(
        jnp.sum(jnp.where(hot[k], gate_values[:, k][:, None], 0.0), axis=0) for k in range(TOPK)
    )

    own_sent = to_owner(product_tn(hot_any, normed_mid).astype(BF))
    mid_group = lax.all_gather(normed_mid, "shard", axis=0, tiled=True)
    mid_group, own_sent = in_order(mid_group, own_sent)
    expert_rows = lax.all_gather(own_sent, "shard", axis=1, tiled=True)
    gate_rows = jnp.broadcast_to(
        slot_gate.reshape(N_EXPERT, 1, SLOT)[:, :, : EXP_DEV * CAP],
        (N_EXPERT, N_SHARD, EXP_DEV * CAP),
    ).reshape(N_EXPERT * N_SHARD, EXP_DEV * CAP)
    gate_rows = lax.all_to_all(
        gate_rows, ("expert", "shard"), split_axis=0, concat_axis=0, tiled=True
    )
    gate_rows = (
        gate_rows.reshape(N_EXPERT, N_SHARD, EXP_DEV, CAP)
        .transpose(2, 1, 0, 3)
        .reshape(EXP_DEV, N_SHARD * N_EXPERT * CAP, 1)
    )

    mid_sent = in_turn(mid_group, gate_rows)
    shared_ab = product(mid_sent, gate_up_w)
    shared_a = shared_ab[:, :hid]
    shared_b = shared_ab[:, hid:]
    silu_shared, slope_shared = silu_parts(shared_a)
    shared_hidden = (silu_shared * shared_b).astype(BF)
    shared_part = product(shared_hidden, down_w).astype(BF)
    expert_first, cot_sent = in_order(
        zero_after(peek(expert_rows, zero_after(gate_rows, shared_part))), cotangent
    )
    cot_group = lax.all_gather(cot_sent, "shard", axis=0, tiled=True)

    both_pre = jnp.einsum("jsd,jfd->jsf", expert_rows, w_expert_both, preferred_element_type=F32)
    gate_pre = both_pre[..., :hid]
    up_pre = both_pre[..., hid:]
    silu_gate, slope_gate = silu_parts(gate_pre)
    expert_hidden = (silu_gate * up_pre).astype(BF)
    expert_hidden = expert_hidden + expert_first.astype(BF)
    hidden_grad = gate_rows * jnp.einsum(
        "jsd,jfd->jsf", expert_cot, w_expert_down, preferred_element_type=F32
    )
    gate_part = jnp.sum(expert_hidden.astype(F32) * hidden_grad, axis=-1)
    grad_gate_pre = (hidden_grad * up_pre * slope_gate).astype(BF)
    grad_up_pre = (hidden_grad * silu_gate).astype(BF)
    row_part = jnp.einsum(
        "jsf,jfd->jsd",
        jnp.concatenate([grad_gate_pre, grad_up_pre], axis=2),
        w_expert_both,
        preferred_element_type=F32,
    ).astype(BF)
    row_own = lax.psum_scatter(row_part, "shard", scatter_dimension=1, tiled=True)
    gate_sent = (
        gate_part.reshape(EXP_DEV, N_SHARD, N_EXPERT, CAP)
        .transpose(2, 1, 0, 3)
        .reshape(N_EXPERT * N_SHARD, EXP_DEV * CAP)
    )
    gate_got = lax.all_to_all(
        gate_sent, ("expert", "shard"), split_axis=0, concat_axis=0, tiled=True
    )
    gate_sum = jnp.sum(gate_got.reshape(N_EXPERT, N_SHARD, EXP_DEV * CAP), axis=1)
    gate_slots = jnp.pad(gate_sum, ((0, 0), (0, SLOT - EXP_DEV * CAP))).reshape(-1)
    gate_times_grad = jnp.stack(
        [jnp.sum(jnp.where(hot[k], gate_slots[None, :], 0.0), axis=1) for k in range(TOPK)], axis=1
    )

    gate_total = jnp.sum(gate_times_grad, axis=1, keepdims=True)
    chosen_grad = (gate_times_grad - gate_values * (gate_total / ROUTE_SCALE)) * (
        1.0 - scores_sig
    )
    logit_grad = jnp.sum(route_hot * chosen_grad[:, :, None], axis=1).astype(BF)

    shared_hidden_grad = product_nt(cot_group, down_w)
    grad_shared_ab = jnp.concatenate(
        [shared_hidden_grad * shared_b * slope_shared, shared_hidden_grad * silu_shared], axis=1
    ).astype(BF)
    shared_row_part = product_nt(grad_shared_ab, gate_up_w).astype(BF)
    gate_up_sum = sum_over_expert(
        jnp.concatenate(
            [
                product_tn(mid_sent, grad_shared_ab).astype(BF),
                product_tn(normed_mid, logit_grad).astype(BF),
            ],
            axis=1,
        ).reshape(N_EXPERT, 128, 2 * hid + expert_count)
    )
    row_own = in_turn(row_own, gate_got, gate_up_sum)
    row_own, shared_row_part = in_order(row_own, shared_row_part)
    shared_row = lax.psum_scatter(shared_row_part, "shard", scatter_dimension=0, tiled=True)
    row_back = from_owner(row_own)

    grad_routes = product(hot_any.astype(BF), row_back)
    grad_top = cotangent.astype(F32)
    normed_grad = product_nt(logit_grad, router_w) + shared_row.astype(F32) + grad_routes
    middle_norm_grad, grad_gain_ffn = rms_backward(middle, inverse_mid, gain_ffn, normed_grad)
    middle_grad = grad_top + middle_norm_grad
    attn_grad = middle_grad.astype(BF)
    grad_group = lax.all_gather(attn_grad, "shard", axis=0, tiled=True)
    ffn_got = lax.all_to_all(
        in_turn(gate_up_sum, attn_grad).astype(BF),
        "shard",
        split_axis=0,
        concat_axis=0,
        tiled=True,
    )
    ffn_got = ffn_got.reshape(N_SHARD, 16, 2 * hid + expert_count).astype(F32)
    expert_part = jnp.einsum(
        "jsf,jfd->jsd",
        in_turn(expert_hidden, attn_grad),
        w_expert_down,
        preferred_element_type=F32,
    ).astype(BF)
    expert_own = lax.psum_scatter(expert_part, "shard", scatter_dimension=1, tiled=True)
    down_sent = jnp.pad(
        product_tn(in_turn(shared_hidden, attn_grad), cot_group)
        .astype(BF)
        .reshape(N_EXPERT, 11, width),
        ((0, 0), (0, 5), (0, 0)),
    )
    mixed = [in_turn(one, expert_part, ffn_got, down_sent) for one in mixed]

    attended_grad = product_nt(grad_group, out_w).astype(BF)
    out_sum = sum_over_expert(
        product_tn(attended, grad_group)
        .astype(BF)
        .reshape(N_EXPERT, 16, width)
    )
    query_grads = []
    expanded_grads = []
    rope_grad = 0.0
    for h in range(HEADS):
        a_h = attended_grad[:, h * DV : (h + 1) * DV]
        inner = in_turn(jnp.sum(mixed[h] * a_h.astype(F32), axis=-1, keepdims=True), out_sum)
        probs_grad = product_nt(a_h, values[h])
        score_grad = (probs_low[h].astype(F32) * (probs_grad - inner)).astype(BF)
        value_grad = product_tn(probs_low[h], a_h)
        query_grad = product(score_grad, keys[h]) * factor
        key_grad = product_tn(score_grad, queries[h]) * factor
        query_grads.append(query_grad[:, :DN])
        query_grads.append(rotate(query_grad[:, DN:], cosine, -sine))
        expanded_grads.append(key_grad[:, :DN])
        expanded_grads.append(value_grad)
        rope_grad = rope_grad + key_grad[:, DN:]
    down_sum = sum_over_expert(in_turn(down_sent, out_sum))
    expanded_grad = jnp.concatenate(expanded_grads, axis=1).astype(BF)
    inverse_latent = lax.rsqrt(
        jnp.mean(compressed * compressed, axis=-1, keepdims=True) + EPSILON
    )
    compressed_grad, _ = rms_backward(
        compressed, inverse_latent, gain_latent, product_nt(expanded_grad, expand_w)
    )
    compressed_grad = in_turn(compressed_grad, down_sum)
    projected_grad = jnp.concatenate(
        query_grads + [compressed_grad, rotate(rope_grad, cosine, -sine)], axis=1
    ).astype(BF)

    ffn_gain = jnp.pad(grad_gain_ffn.reshape(N_EXPERT, 128, 1), ((0, 0), (0, 0), (64, 63)))
    normed_part = product_nt(projected_grad, query_latent_w).astype(BF)
    expert_own, normed_part = in_order(expert_own, normed_part)
    normed_in_grad = lax.psum_scatter(normed_part, "shard", scatter_dimension=0, tiled=True)
    expert_back = from_owner(expert_own)
    grads_sent, latent_sent = owner_grads(
        normed_in,
        projected_grad,
        product_tn(latent_normed, expanded_grad).astype(BF).reshape(N_EXPERT, 128, 128),
        in_turn(ffn_gain, normed_part, expert_back),
    )
    grads_sum = sum_over_expert(grads_sent)
    latent_own = lax.psum_scatter(
        latent_sent.reshape(N_SHARD * N_EXPERT * 16, 640),
        "shard",
        scatter_dimension=0,
        tiled=True,
    )
    normed_in_grad, shared_part = in_order(normed_in_grad, shared_part)
    shared_out = lax.psum_scatter(shared_part, "shard", scatter_dimension=0, tiled=True)
    grads_got = lax.all_to_all(
        grads_sum.astype(BF), "shard", split_axis=0, concat_axis=0, tiled=True
    )
    grads_got = grads_got.reshape(N_SHARD, 16, QW + 128).astype(F32)
    latent_sum = sum_over_expert(latent_own.reshape(N_EXPERT, 16, 640))
    turned_back = lax.ppermute(
        in_turn(jnp.concatenate([out_sum, down_sum], axis=0), grads_sum).astype(BF),
        ("expert", "shard"),
        back_pairs,
    ).astype(F32)

    grad_expert_down = jnp.einsum(
        "jsf,jsd->jfd",
        in_turn((expert_hidden.astype(F32) * gate_rows).astype(BF), grads_sent),
        expert_cot,
        preferred_element_type=F32,
    )
    grad_expert_gate = jnp.einsum(
        "jsf,jsd->jfd",
        in_turn(grad_gate_pre, grads_sent),
        expert_rows,
        preferred_element_type=F32,
    )
    grad_expert_up = jnp.einsum(
        "jsf,jsd->jfd",
        in_turn(grad_up_pre, grads_sent),
        expert_rows,
        preferred_element_type=F32,
    )

    normed_in_grad = normed_in_grad.astype(F32)
    inverse_in = lax.rsqrt(jnp.mean(inputs32 * inputs32, axis=-1, keepdims=True) + EPSILON)
    input_norm_grad, _ = rms_backward(
        inputs32, inverse_in, gain_attn, normed_in_grad
    )
    grad_input = middle_grad + input_norm_grad

    route_out = [product(hot[k].astype(BF), expert_back) for k in range(TOPK)]
    mixture = sum(gate_values[:, k][:, None] * route_out[k] for k in range(TOPK))
    layer_out = (middle + shared_out.astype(F32) + mixture).astype(BF)

    grad_shared_gate = ffn_got[:, :, :hid].transpose(1, 0, 2).reshape(16, N_SHARD * hid)
    grad_shared_up = (
        ffn_got[:, :, hid : 2 * hid].transpose(1, 0, 2).reshape(16, N_SHARD * hid)
    )
    grad_router_own = jnp.sum(ffn_got[:, :, 2 * hid :], axis=0)
    grad_shared_down = turned_back[16:27]
    grad_out_own = turned_back[:16]

    query_own = grads_got[:, :, :QW].transpose(1, 0, 2).reshape(16, N_SHARD * QW)
    grad_expand_own = (
        grads_got[:, :, QW : QW + 128]
        .reshape(N_SHARD, 4, KVW // 128, 128)
        .transpose(1, 0, 2, 3)
        .reshape(4, N_SHARD * KVW)
    )
    grad_latent_own = latent_sum[:, :LW]
    grad_norm_ffn = latent_sum[:, LW]
    grad_norm_attn = (
        jnp.sum(w_query.astype(F32) * query_own, axis=1)
        + jnp.sum(w_latent.astype(F32) * grad_latent_own, axis=1)
    ) / norm_attn.astype(F32)
    grad_norm_latent = jnp.sum(w_expand.astype(F32) * grad_expand_own, axis=1) / (
        norm_latent.astype(F32)
    )

    return (
        layer_out,
        grad_input,
        grad_norm_attn,
        query_own,
        grad_latent_own,
        grad_norm_latent,
        grad_expand_own,
        grad_out_own,
        grad_norm_ffn,
        grad_router_own,
        grad_shared_gate,
        grad_shared_up,
        grad_shared_down,
        grad_expert_gate,
        grad_expert_up,
        grad_expert_down,
    )


def solution(mesh):
    both = P(("expert", "shard"), None)
    vector = P(("expert", "shard"))
    groups = P("expert", None)
    experts = P("expert", "shard", None)
    return jax.shard_map(
        body,
        mesh=mesh,
        in_specs=(
            both,
            both,
            groups,
            groups,
            both,
            vector,
            both,
            both,
            vector,
            both,
            both,
            vector,
            both,
            both,
            both,
            both,
            experts,
            experts,
            experts,
        ),
        out_specs=(
            both,
            both,
            vector,
            both,
            both,
            vector,
            both,
            both,
            vector,
            both,
            both,
            both,
            both,
            experts,
            experts,
            experts,
        ),
        check_vma=False,
    )
```
